128 devices in a mesh: seq: 64 (over y, x, z_hi, core), fsdp: 2 (over z_lo).
Axes of the slice: x: 4, y: 4, z: 4 (z_hi: 2, z_lo: 2; z = z_hi * 2 + z_lo), core: 2. Of those that a mesh axis runs over, the one named last changes fastest.
Arguments:
- block_input: float32 [2, 8192, 1024], P('fsdp', 'seq'), may hold values from -6 to 6
- norm_gain: bfloat16 [1024], P(('seq', 'fsdp')), may hold values from 0.3984375 to 1.59375
- in_weight: bfloat16 [1024, 3072], P(('seq', 'fsdp')), may hold values from -0.1875 to 0.1875
- conv_taps: bfloat16 [1024, 3], P(('seq', 'fsdp')), may hold values from -3 to 3
- out_weight: bfloat16 [1024, 1024], P(('seq', 'fsdp')), may hold values from -0.1875 to 0.1875
- ffn_gain: bfloat16 [1024], P(('seq', 'fsdp')), may hold values from 0.3984375 to 1.59375
- gate_weight: bfloat16 [1024, 4608], P(('seq', 'fsdp')), may hold values from -0.1875 to 0.1875
- up_weight: bfloat16 [1024, 4608], P(('seq', 'fsdp')), may hold values from -0.1875 to 0.1875
- down_weight: bfloat16 [4608, 1024], P(('seq', 'fsdp')), may hold values from -0.1875 to 0.1875
- out_cotangent: float32 [2, 8192, 1024], P('fsdp', 'seq'), may hold values from -6 to 6
Outputs:
- block_output: float32 [2, 8192, 1024], P('fsdp', 'seq')
- input_grad: float32 [2, 8192, 1024], P('fsdp', 'seq')
- norm_gain_grad: float32 [1024], P(('seq', 'fsdp'))
- in_weight_grad: float32 [1024, 3072], P(('seq', 'fsdp'))
- conv_taps_grad: float32 [1024, 3], P(('seq', 'fsdp'))
- out_weight_grad: float32 [1024, 1024], P(('seq', 'fsdp'))
- ffn_gain_grad: float32 [1024], P(('seq', 'fsdp'))
- gate_weight_grad: float32 [1024, 4608], P(('seq', 'fsdp'))
- up_weight_grad: float32 [1024, 4608], P(('seq', 'fsdp'))
- down_weight_grad: float32 [4608, 1024], P(('seq', 'fsdp'))
The draws below stay inside these ranges and needn't reach their ends.
All inputs are finite; a program needn't handle non-finite values.
Results may differ from the reference program's by a relative error of at most 0.0096.
Values may be sent and summed in bfloat16 or wider, within the bound.
No kernel may reach another device: no remote copies, remote signals or barrier semaphores. Data moves between devices by JAX's collectives and lax.ppermute only.
A program may use at most 192 MiB of HBM per device.

```python
import jax
import jax.numpy as jnp
from jax import lax

D = 1024
FF = 4608
LENGTH = 8192
SEQS = 2


def steps_of(rng, shape, split, least, high):
    level, own = 1.0, jax.random.fold_in(rng, 6)
    for axis_at, blocks in split:
        draws = jnp.exp(jax.random.uniform(jax.random.fold_in(own, axis_at), (blocks,), jnp.float32, least / len(split), high / len(split)))
        level = level * jnp.repeat(draws, shape[axis_at] // blocks).reshape([-1 if axis == axis_at else 1 for axis in range(len(shape))])
    return level


def normal_values(stream_key, dims, spread, reach, split=(), kind=jnp.bfloat16):
    array = spread * jax.random.normal(stream_key, dims, jnp.float32)
    if split:
        array = array * steps_of(stream_key, dims, split, -0.22, 0.18)
    return jnp.clip(array, -reach, reach).astype(kind)


def setup_inputs(seed: int = 0) -> dict:
    key_list = jax.random.split(jax.random.key(seed), 11)
    return {
        "block_input": normal_values(key_list[0], (SEQS, LENGTH, D), 1.0, 6.0, ((0, 2), (1, 64)), jnp.float32),
        "norm_gain": jnp.clip(1.0 + 0.12 * jax.random.normal(key_list[1], (D,), jnp.float32), 0.3984375, 1.59375).astype(jnp.bfloat16),
        "in_weight": normal_values(key_list[2], (D, 3 * D), D ** -0.5, 0.1875, ((0, 128),)),
        "conv_taps": normal_values(key_list[3], (D, 3), 0.6, 3.0, ((0, 128),)),
        "out_weight": normal_values(key_list[4], (D, D), D ** -0.5, 0.1875, ((0, 128),)),
        "ffn_gain": jnp.clip(1.0 + 0.12 * jax.random.normal(key_list[5], (D,), jnp.float32), 0.3984375, 1.59375).astype(jnp.bfloat16),
        "gate_weight": normal_values(key_list[6], (D, FF), D ** -0.5, 0.1875, ((0, 128),)),
        "up_weight": normal_values(key_list[7], (D, FF), D ** -0.5, 0.1875, ((0, 128),)),
        "down_weight": normal_values(key_list[8], (FF, D), (FF // 4) ** -0.5, 0.1875, ((0, 128),)),
        "out_cotangent": normal_values(key_list[9], (SEQS, LENGTH, D), 1.0, 6.0, ((0, 2), (1, 64)), jnp.float32),
    }


EPS = 1e-05

@jax.custom_vjp
def low(v):
    return lax.optimization_barrier(v.astype(jnp.bfloat16)).astype(jnp.float32)

@jax.custom_vjp
def low_back(v):
    return v

def low_keep(v):
    return (low(v), None)

def low_pass(kept, grad):
    return (grad,)

def back_keep(v):
    return (v, None)

def back_low(kept, grad):
    return (low(grad),)
low.defvjp(low_keep, low_pass)
low_back.defvjp(back_keep, back_low)

def product(left, right):
    return jnp.dot(left, right, precision=lax.Precision.HIGHEST)

def rms_scale(rows, gain):
    return rows * lax.rsqrt(lax.optimization_barrier(jnp.mean(rows * rows, axis=-1, keepdims=True)) + EPS) * gain

def forward(rows_in, norm_gain, in_weight, conv_taps, out_weight, ffn_gain, gate_weight, up_weight, down_weight):
    width = rows_in.shape[1]
    normed_one = low(rms_scale(rows_in, norm_gain))
    mixed = low_back(product(normed_one, in_weight))
    gate_b = mixed[:, :width]
    gate_c = mixed[:, width:2 * width]
    values = mixed[:, 2 * width:]
    gated = gate_b * values
    blank = jnp.zeros((2, width), jnp.float32)
    extended = jnp.concatenate([blank, gated], axis=0)
    conv = conv_taps[:, 0] * extended[:-2] + conv_taps[:, 1] * extended[1:-1] + conv_taps[:, 2] * extended[2:]
    mixer = low(gate_c * conv)
    branch = low_back(product(mixer, out_weight))
    hidden = rows_in + branch
    normed_two = low(rms_scale(hidden, ffn_gain))
    gate_pre = low_back(product(normed_two, gate_weight))
    up_pre = low_back(product(normed_two, up_weight))
    act = low(jax.nn.silu(gate_pre) * up_pre)
    ffn_out = low_back(product(act, down_weight))
    return hidden + ffn_out

def reference(block_input, norm_gain, in_weight, conv_taps, out_weight, ffn_gain, gate_weight, up_weight, down_weight, out_cotangent):
    params = tuple((p.astype(jnp.float32) for p in (norm_gain, in_weight, conv_taps, out_weight, ffn_gain, gate_weight, up_weight, down_weight)))
    zeroes = tuple((jnp.zeros(p.shape, jnp.float32) for p in params))

    def one_sequence(totals, item):
        seq_rows, seq_cot = item
        result, pullback = jax.vjp(forward, seq_rows, *params)
        grads = pullback(seq_cot)
        new_totals = tuple((t + g for t, g in zip(totals, grads[1:])))
        return (new_totals, (result, grads[0]))
    totals, (outputs, input_grad) = lax.scan(one_sequence, zeroes, (block_input, out_cotangent))
    return (outputs, input_grad, totals[0], totals[1], totals[2], totals[3], totals[4], totals[5], totals[6], totals[7])
```

```python
import jax
import jax.numpy as jnp
import numpy as np
from jax import lax
from jax.sharding import Mesh, PartitionSpec as P

EPS = 1e-05
AXES = ("y", "x", "zh", "core", "zl")
DIMS = (4, 4, 2, 2, 2)
PLANE = ("y", "x")
BOX = ("zh", "core", "zl")
RING = ("zh", "zl")
BF = jnp.bfloat16
F32 = jnp.float32


def dot(left, right, dims, kind=F32):
    out = lax.dot_general(left, right, (dims, ((), ())), preferred_element_type=F32)
    return out.astype(kind)


def row(left, right, kind=F32):
    return dot(left, right, ((1,), (0,)), kind)


def row_back(left, right, kind=F32):
    return dot(left, right, ((1,), (1,)), kind)


def col_sum(left, right):
    return dot(left, right, ((0,), (0,)), BF)


def after(value, other):
    mark = other[tuple(size - 1 for size in other.shape)]
    return value * jnp.where(mark == mark, 1.0, 0.0).astype(value.dtype)


def swap(value):
    return lax.ppermute(value, "core", [(0, 1), (1, 0)])


def turn(value, by):
    return lax.ppermute(value, RING, [(i, (i + by) % 4) for i in range(4)])


def send(value, axes):
    return lax.all_to_all(value, axes, 0, 0, tiled=True)


def ring_place():
    return lax.axis_index("zh") * 2 + lax.axis_index("zl")


def everyone(value):
    rows = value.shape[0]
    cut, me = rows // 2, ring_place()
    above, below = turn(value, 1), turn(value, 3)
    far = [turn(above[:cut], 1), turn(below[cut:], 3)]
    ring = jnp.zeros((4 * rows,) + value.shape[1:], value.dtype)
    for block, by, start in (
        (value, 0, 0),
        (below, 1, 0),
        (above, 3, 0),
        (far[0], 2, 0),
        (far[1], 2, cut),
    ):
        ring = lax.dynamic_update_slice_in_dim(ring, block, (me + by) % 4 * rows + start, 0)
    return jnp.concatenate([ring, swap(ring)], axis=0)


def mine(keep, give, kind=BF):
    rows = keep.shape[0] // 4
    cut, me = rows // 2, ring_place()
    ring = keep + swap(give.astype(kind)).astype(F32)

    def part(by, start, size):
        return lax.dynamic_slice_in_dim(ring, (me + by) % 4 * rows + start, size, 0)

    from_left = turn(part(2, 0, cut).astype(kind), 1).astype(F32)
    from_right = turn(part(2, cut, cut).astype(kind), 3).astype(F32)
    to_right = jnp.concatenate([part(1, 0, cut) + from_left, part(1, cut, cut)], axis=0)
    to_left = jnp.concatenate([part(3, 0, cut), part(3, cut, cut) + from_right], axis=0)
    one, two = turn(to_right.astype(kind), 1), turn(to_left.astype(kind), 3)
    return part(0, 0, rows) + one.astype(F32) + two.astype(F32)


def mine_both(left, right, other):
    rows = left[0].shape[0] // 4
    cut, me = rows // 2, ring_place()
    rings = [
        keep + swap(give).astype(F32) for keep, give in (left, right)
    ]

    def part(by, start, size):
        at = (me + by) % 4 * rows + start
        return jnp.concatenate([lax.dynamic_slice_in_dim(r, at, size, 0) for r in rings], axis=1)

    from_left = turn(after(part(2, 0, cut).astype(BF), other), 1).astype(F32)
    from_right = turn(after(part(2, cut, cut).astype(BF), other), 3).astype(F32)
    to_right = jnp.concatenate([part(1, 0, cut) + from_left, part(1, cut, cut)], axis=0)
    to_left = jnp.concatenate([part(3, 0, cut), part(3, cut, cut) + from_right], axis=0)
    one, two = turn(to_right.astype(BF), 1), turn(to_left.astype(BF), 3)
    total = part(0, 0, rows) + one.astype(F32) + two.astype(F32)
    return total[:, :1024], total[:, 1024:]


def channel_order(width):
    natural, place = np.arange(width)[:, None], np.arange(width)[None, :]
    wanted = natural // 8 % 8 * (width // 8) + natural // 64 * 8 + natural % 8
    return jnp.asarray((wanted == place).astype(BF))


def unit_order():
    natural, place = np.arange(1152)[:, None], np.arange(1280)[None, :]
    p, e, r = natural // 288, natural // 36 % 8, natural % 36
    wanted = np.where(r < 32, e * 128 + p * 32 + r, 992 + e * 32 + p * 8 + r)
    return jnp.asarray((wanted == place).astype(BF))


def stacked(value):
    rows = value.shape[0]
    return value.reshape(rows // 8, 8, 8, 128).transpose(0, 2, 1, 3).reshape(rows * 8, 128)


def spread(value):
    rows = value.shape[0] // 8
    return value.reshape(rows // 8, 8, 8, 128).transpose(0, 2, 1, 3).reshape(rows, 1024)


def on_device(
    block_input,
    norm_gain,
    in_weight,
    conv_taps,
    out_weight,
    ffn_gain,
    gate_weight,
    up_weight,
    down_weight,
    out_cotangent,
):
    width = in_weight.shape[1] // 3
    ch = width // 8
    core = lax.axis_index("core")
    zh = lax.axis_index("zh")
    zl = lax.axis_index("zl")
    member = zh * 4 + core * 2 + zl
    x = block_input.reshape(-1, width)
    cot = out_cotangent.reshape(-1, width)
    rows = x.shape[0]
    shard = out_weight.shape[0]

    def box_rows(value):
        both = lax.all_gather(value, ("core",) + RING, axis=0, tiled=True)
        half = 4 * value.shape[0]
        return jnp.where(core == 0, both, jnp.concatenate([both[half:], both[:half]], axis=0))

    order = channel_order(width)
    units = unit_order()
    marks = jnp.concatenate([jnp.stack([norm_gain, ffn_gain], axis=1), conv_taps], axis=1)
    marks = jnp.pad(marks, ((0, 0), (0, 123)))
    in_cols = row(in_weight.reshape(-1, width), order, BF).reshape(shard, 3, 8, ch)
    gu_cols = jnp.concatenate([gate_weight, up_weight], axis=0).reshape(8 * shard, 1152)
    gu_cols = row(gu_cols, units, BF).reshape(2, shard, 4, 1280)
    most = gu_cols[..., :1024].reshape(2, shard, 4, 8, 128).transpose(3, 1, 0, 2, 4)
    rest = gu_cols[..., 1024:].reshape(2, shard, 4, 8, 32).transpose(3, 1, 0, 2, 4)
    gu_cols = jnp.concatenate(
        [most.reshape(8, shard, 2, 512), rest.reshape(8, shard, 2, 128)], axis=3
    )
    pack = jnp.concatenate(
        [
            in_cols.transpose(2, 0, 1, 3).reshape(8, shard, 3 * ch),
            jnp.broadcast_to(marks, (8,) + marks.shape),
            gu_cols.reshape(8, shard, 1280),
        ],
        axis=2,
    )
    cols = send(pack, BOX).reshape(8 * shard, -1)
    down_most = down_weight[:32]
    down_rest = jnp.pad(down_weight[32:], ((0, 4), (0, 0)))
    ffn_w = lax.all_gather(
        jnp.concatenate(
            [
                cols[:, 512:],
                jnp.concatenate([down_most[:, :512], down_most[:, 512:]], axis=0),
                stacked(down_rest),
            ],
            axis=1,
        ),
        PLANE,
        axis=0,
        tiled=True,
    )
    slot = jnp.concatenate([cols[:, :512], stacked(out_weight)], axis=1)
    mixer_w = send(jnp.broadcast_to(slot, (16,) + slot.shape), PLANE).reshape(width, -1)
    w_in = mixer_w[:, : 3 * ch]
    w_out = spread(mixer_w[:, 512:])
    mark_rows = row_back(jnp.eye(8, 128, dtype=BF), mixer_w[:, 384:512])
    gain_one, gain_two = mark_rows[0], mark_rows[1]
    taps = row(mark_rows.astype(BF), order)[2:5]
    taps = lax.dynamic_slice_in_dim(taps, member * ch, ch, axis=1)

    inv_one = lax.rsqrt(jnp.mean(x * x, axis=-1, keepdims=True) + EPS)
    scaled = x * inv_one
    high = lax.reduce_precision(scaled, 8, 7)
    high, low = high.astype(BF), (scaled - high).astype(BF)
    scaled_all = box_rows(jnp.concatenate([high, low], axis=1))
    scaled_all = scaled_all[:, :width].astype(F32) + scaled_all[:, width:].astype(F32)
    cot_all = everyone(after(cot.astype(BF), cols))
    n1 = (scaled_all * after(gain_one, cot_all)).astype(BF)
    mixed = row(n1, w_in)
    gate_b, gate_c, values = mixed[:, :ch], mixed[:, ch : 2 * ch], mixed[:, 2 * ch :]
    gated = gate_b * values

    place = jnp.arange(8)
    its_z = place % 4
    its_core = jnp.where(place < 4, core, 1 - core)
    its_seq, its_turn = its_z % 2, its_z // 2 * 2 + its_core
    same = its_seq[:, None] == its_seq[None, :]
    before = (same & (its_turn[:, None] == its_turn[None, :] + 1)).astype(F32)
    behind = (same & (its_turn[:, None] + 1 == its_turn[None, :])).astype(F32)
    seqs = jnp.arange(2)
    first = ((seqs[:, None] == its_seq[None, :]) & (its_turn[None, :] == 0)).astype(F32)
    last = ((seqs[:, None] == its_seq[None, :]) & (its_turn[None, :] == 3)).astype(F32)

    def pick(table, value):
        return jnp.sum(table[:, :, None, None] * value[None], axis=1)

    def blocks(value):
        return value.reshape(8, rows, -1)

    def halves(product, left, right):
        cut = 4 * rows
        give = product(left[cut:], right, BF)
        return product(left[:cut], right), give

    def flat(value):
        return value.reshape(8 * rows, -1)

    line = [(i, i + 1) for i in range(15)]
    gated_b = blocks(gated)
    ends = gated_b[:, rows - 2 :]
    carried = lax.ppermute(pick(last, ends), PLANE, line)
    heads = pick(before, ends) + pick(first.T, carried)
    late2 = flat(jnp.concatenate([heads, gated_b[:, : rows - 2]], axis=1))
    late1 = flat(jnp.concatenate([heads[:, 1:], gated_b[:, : rows - 1]], axis=1))
    conv = taps[0] * late2 + taps[1] * late1 + taps[2] * gated
    mixer = (gate_c * conv).astype(BF)
    hidden = x + mine(*halves(row, mixer, w_out))
    inv_two = lax.rsqrt(jnp.mean(hidden * hidden, axis=-1, keepdims=True) + EPS)
    n2 = everyone((hidden * inv_two * gain_two).astype(BF))
    w_gu = ffn_w[:, :1280]
    down_most = ffn_w[:, 1280:1792].reshape(16, 2, 32, 512).transpose(0, 2, 1, 3)
    w_down = jnp.concatenate(
        [down_most.reshape(512, width), spread(ffn_w[:, 1792:])], axis=0
    )
    gu = row(n2, w_gu)
    gate_pre, up_pre = gu[:, :640], gu[:, 640:]
    sigma = jax.nn.sigmoid(gate_pre)
    act = (gate_pre * sigma * up_pre).astype(BF)

    grad_act = row_back(cot_all, w_down)
    grad_up_pre = (grad_act * gate_pre * sigma).astype(BF)
    grad_gate_pre = (grad_act * up_pre * sigma * (1.0 + gate_pre * (1.0 - sigma))).astype(BF)
    grad_gu_pre = jnp.concatenate([grad_gate_pre, grad_up_pre], axis=1)
    gn2_part = row_back(grad_gu_pre, w_gu)
    gn2 = mine(gn2_part[: 4 * rows], gn2_part[4 * rows :])
    down_terms = col_sum(act, cot_all)
    down_most = down_terms[:512].reshape(16, 32, 2, 512).transpose(0, 2, 1, 3)
    ffn_sums = jnp.concatenate(
        [col_sum(n2, grad_gu_pre), down_most.reshape(width, 512), stacked(down_terms[512:])],
        axis=1,
    )
    ffn_sums_y = lax.psum_scatter(ffn_sums, "y", scatter_dimension=0, tiled=True)
    ffn_sums = lax.psum_scatter(ffn_sums_y, "x", scatter_dimension=0, tiled=True)
    gain_two_term = jnp.sum(gn2 * hidden * inv_two, axis=0)
    weighted = gn2 * gain_two
    grad_hidden = (
        cot
        + inv_two * weighted
        - hidden * inv_two**3 * jnp.mean(hidden * weighted, axis=-1, keepdims=True)
    )
    hb = everyone(grad_hidden.astype(BF))
    grad_mixer = row_back(hb, w_out)
    grad_c = grad_mixer * conv
    grad_conv = grad_mixer * gate_c
    taps_term = jnp.stack(
        [
            jnp.sum(late2 * grad_conv, axis=0),
            jnp.sum(late1 * grad_conv, axis=0),
            jnp.sum(gated * grad_conv, axis=0),
        ],
        axis=0,
    )
    gc = blocks(grad_conv)
    starts = gc[:, :2]
    from_next = lax.ppermute(pick(first, starts), PLANE, [(b, a) for a, b in line])
    tails = pick(behind, starts) + pick(last.T, from_next)
    lead1 = flat(jnp.concatenate([gc[:, 1:], tails[:, :1]], axis=1))
    lead2 = flat(jnp.concatenate([gc[:, 2:], tails], axis=1))
    grad_gated = taps[2] * grad_conv + taps[1] * lead1 + taps[0] * lead2
    grad_mixed = jnp.concatenate(
        [grad_gated * values, grad_c, grad_gated * gate_b], axis=1
    ).astype(BF)
    keep, give = halves(row_back, grad_mixed, w_in)
    gain_one_term = jnp.sum(keep * scaled_all[: 4 * rows], axis=0)
    gain_one_term += jnp.sum(give.astype(F32) * scaled_all[4 * rows :], axis=0)
    taps_all = jnp.where(jnp.arange(width) // ch == member, jnp.tile(taps_term, (1, 8)), 0.0)
    taps_all = row_back(taps_all.astype(BF), order)
    mark_terms = jnp.concatenate([gain_one_term[None], gain_two_term[None], taps_all], axis=0)
    mark_terms = jnp.pad(mark_terms, ((0, 3), (0, 0))).T
    mark_terms = jnp.pad(mark_terms, ((0, 0), (0, 120))).astype(BF)
    in_terms = col_sum(n1, grad_mixed)
    mixer_terms = jnp.concatenate(
        [in_terms, mark_terms, stacked(col_sum(mixer, hb))], axis=1
    )
    parts = send(mixer_terms.reshape(16, 64, -1), PLANE)
    mixer_sums = jnp.sum(parts.astype(F32), axis=0)
    ffn = after(row(act, w_down), hb)
    late = ffn[: 4 * rows], ffn[4 * rows :].astype(BF)
    gn1, ffn = mine_both((keep, after(give, in_terms)), late, ffn_sums_y)
    weighted = gn1 * gain_one
    input_grad = (
        grad_hidden
        + inv_one * weighted
        - x * inv_one**3 * jnp.mean(x * weighted, axis=-1, keepdims=True)
    )
    result = hidden + ffn

    cols = jnp.concatenate([mixer_sums[:, :512].astype(BF), ffn_sums[:, :1280]], axis=1)
    cols = send(cols.reshape(8, shard, -1), BOX)
    in_cols = cols[:, :, : 3 * ch].reshape(8, shard, 3, ch).transpose(1, 2, 0, 3)
    grad_in = row_back(in_cols.reshape(3 * shard, width), order).reshape(shard, 3 * width)
    mark_sums = jnp.sum(cols[:, :, 384:392].astype(F32), axis=0)
    gu_cols = cols[:, :, 512:].reshape(8, shard, 2, 640)
    most = gu_cols[..., :512].reshape(8, shard, 2, 4, 128).transpose(2, 1, 3, 0, 4)
    rest = gu_cols[..., 512:].reshape(8, shard, 2, 4, 32).transpose(2, 1, 3, 0, 4)
    gu_cols = jnp.concatenate(
        [most.reshape(8 * shard, 1024), rest.reshape(8 * shard, 256)], axis=1
    )
    grad_gate, grad_up = row_back(gu_cols, units).reshape(2, shard, 4608)
    down_most = ffn_sums[:, 1280:1792]
    grad_down = jnp.concatenate(
        [
            jnp.concatenate([down_most[:32], down_most[32:]], axis=1),
            spread(ffn_sums[:, 1792:])[:4],
        ],
        axis=0,
    ).astype(F32)
    shape_rows = block_input.shape
    return (
        result.reshape(shape_rows),
        input_grad.reshape(shape_rows),
        mark_sums[:, 0],
        grad_in,
        mark_sums[:, 2:5],
        spread(mixer_sums[:, 512:]),
        mark_sums[:, 1],
        grad_gate,
        grad_up,
        grad_down,
    )


def solution(mesh):
    torus = Mesh(mesh.devices.reshape(DIMS), AXES)
    line = P("zl", ("y", "x", "zh", "core"), None)
    flat, table = P(AXES), P(AXES, None)
    return jax.shard_map(
        on_device,
        mesh=torus,
        in_specs=(line, flat, table, table, table, flat, table, table, table, line),
        out_specs=(line, line, flat, table, table, table, flat, table, table, table),
        check_vma=False,
    )
```

```python
import jax
import jax.numpy as jnp
import numpy as np
from jax import lax
from jax.sharding import Mesh, PartitionSpec as P

EPS = 1e-05
AXES = ("y", "x", "zh", "core", "zl")
DIMS = (4, 4, 2, 2, 2)
PLANE = ("y", "x")
BOX = ("zh", "core", "zl")
RING = ("zh", "zl")
BF = jnp.bfloat16
F32 = jnp.float32


def dot(left, right, dims, kind=F32):
    out = lax.dot_general(left, right, (dims, ((), ())), preferred_element_type=F32)
    return out.astype(kind)


def row(left, right, kind=F32):
    return dot(left, right, ((1,), (0,)), kind)


def row_back(left, right, kind=F32):
    return dot(left, right, ((1,), (1,)), kind)


def col_sum(left, right):
    return dot(left, right, ((0,), (0,)), BF)


def after(value, other):
    mark = other[tuple(size - 1 for size in other.shape)]
    return value * jnp.where(mark == mark, 1.0, 0.0).astype(value.dtype)


def swap(value):
    return lax.ppermute(value, "core", [(0, 1), (1, 0)])


def turn(value, by):
    return lax.ppermute(value, RING, [(i, (i + by) % 4) for i in range(4)])


def send(value, axes):
    return lax.all_to_all(value, axes, 0, 0, tiled=True)


def ring_place():
    return lax.axis_index("zh") * 2 + lax.axis_index("zl")


def everyone(value):
    rows = value.shape[0]
    cut, me = rows // 2, ring_place()
    above, below = turn(value, 1), turn(value, 3)
    far = [turn(above[:cut], 1), turn(below[cut:], 3)]
    ring = jnp.zeros((4 * rows,) + value.shape[1:], value.dtype)
    for block, by, start in (
        (value, 0, 0),
        (below, 1, 0),
        (above, 3, 0),
        (far[0], 2, 0),
        (far[1], 2, cut),
    ):
        ring = lax.dynamic_update_slice_in_dim(ring, block, (me + by) % 4 * rows + start, 0)
    return jnp.concatenate([ring, swap(ring)], axis=0)


def mine(keep, give, kind=BF):
    rows = keep.shape[0] // 4
    cut, me = rows // 2, ring_place()
    ring = keep + swap(give.astype(kind)).astype(F32)

    def part(by, start, size):
        return lax.dynamic_slice_in_dim(ring, (me + by) % 4 * rows + start, size, 0)

    from_left = turn(part(2, 0, cut).astype(kind), 1).astype(F32)
    from_right = turn(part(2, cut, cut).astype(kind), 3).astype(F32)
    to_right = jnp.concatenate([part(1, 0, cut) + from_left, part(1, cut, cut)], axis=0)
    to_left = jnp.concatenate([part(3, 0, cut), part(3, cut, cut) + from_right], axis=0)
    one, two = turn(to_right.astype(kind), 1), turn(to_left.astype(kind), 3)
    return part(0, 0, rows) + one.astype(F32) + two.astype(F32)


def mine_both(left, right, other):
    rows = left[0].shape[0] // 4
    cut, me = rows // 2, ring_place()
    rings = [
        keep + swap(give).astype(F32) for keep, give in (left, right)
    ]

    def part(by, start, size):
        at = (me + by) % 4 * rows + start
        return jnp.concatenate([lax.dynamic_slice_in_dim(r, at, size, 0) for r in rings], axis=1)

    from_left = turn(after(part(2, 0, cut).astype(BF), other), 1).astype(F32)
    from_right = turn(after(part(2, cut, cut).astype(BF), other), 3).astype(F32)
    to_right = jnp.concatenate([part(1, 0, cut) + from_left, part(1, cut, cut)], axis=0)
    to_left = jnp.concatenate([part(3, 0, cut), part(3, cut, cut) + from_right], axis=0)
    one, two = turn(to_right.astype(BF), 1), turn(to_left.astype(BF), 3)
    total = part(0, 0, rows) + one.astype(F32) + two.astype(F32)
    return total[:, :1024], total[:, 1024:]


def channel_order(width):
    natural, place = np.arange(width)[:, None], np.arange(width)[None, :]
    wanted = natural // 8 % 8 * (width // 8) + natural // 64 * 8 + natural % 8
    return jnp.asarray((wanted == place).astype(BF))


def unit_order():
    natural, place = np.arange(1152)[:, None], np.arange(1280)[None, :]
    p, e, r = natural // 288, natural // 36 % 8, natural % 36
    wanted = np.where(r < 32, e * 128 + p * 32 + r, 992 + e * 32 + p * 8 + r)
    return jnp.asarray((wanted == place).astype(BF))


def stacked(value):
    rows = value.shape[0]
    return value.reshape(rows // 8, 8, 8, 128).transpose(0, 2, 1, 3).reshape(rows * 8, 128)


def spread(value):
    rows = value.shape[0] // 8
    return value.reshape(rows // 8, 8, 8, 128).transpose(0, 2, 1, 3).reshape(rows, 1024)


def on_device(
    block_input,
    norm_gain,
    in_weight,
    conv_taps,
    out_weight,
    ffn_gain,
    gate_weight,
    up_weight,
    down_weight,
    out_cotangent,
):
    width = in_weight.shape[1] // 3
    ch = width // 8
    core = lax.axis_index("core")
    zh = lax.axis_index("zh")
    zl = lax.axis_index("zl")
    member = zh * 4 + core * 2 + zl
    x = block_input.reshape(-1, width)
    cot = out_cotangent.reshape(-1, width)
    rows = x.shape[0]
    shard = out_weight.shape[0]

    def box_rows(value):
        both = lax.all_gather(value, ("core",) + RING, axis=0, tiled=True)
        half = 4 * value.shape[0]
        return jnp.where(core == 0, both, jnp.concatenate([both[half:], both[:half]], axis=0))

    order = channel_order(width)
    units = unit_order()
    marks = jnp.concatenate([jnp.stack([norm_gain, ffn_gain], axis=1), conv_taps], axis=1)
    marks = jnp.pad(marks, ((0, 0), (0, 123)))
    in_cols = row(in_weight.reshape(-1, width), order, BF).reshape(shard, 3, 8, ch)
    gu_cols = jnp.concatenate([gate_weight, up_weight], axis=0).reshape(8 * shard, 1152)
    gu_cols = row(gu_cols, units, BF).reshape(2, shard, 4, 1280)
    most = gu_cols[..., :1024].reshape(2, shard, 4, 8, 128).transpose(3, 1, 0, 2, 4)
    rest = gu_cols[..., 1024:].reshape(2, shard, 4, 8, 32).transpose(3, 1, 0, 2, 4)
    gu_cols = jnp.concatenate(
        [most.reshape(8, shard, 2, 512), rest.reshape(8, shard, 2, 128)], axis=3
    )
    pack = jnp.concatenate(
        [
            in_cols.transpose(2, 0, 1, 3).reshape(8, shard, 3 * ch),
            jnp.broadcast_to(marks, (8,) + marks.shape),
            gu_cols.reshape(8, shard, 1280),
        ],
        axis=2,
    )
    cols = send(pack, BOX).reshape(8 * shard, -1)
    down_most = down_weight[:32]
    down_rest = jnp.pad(down_weight[32:], ((0, 4), (0, 0)))
    ffn_w = lax.all_gather(
        jnp.concatenate(
            [
                cols[:, 512:],
                jnp.concatenate([down_most[:, :512], down_most[:, 512:]], axis=0),
                stacked(down_rest),
            ],
            axis=1,
        ),
        PLANE,
        axis=0,
        tiled=True,
    )
    slot = jnp.concatenate([cols[:, :512], stacked(out_weight)], axis=1)
    mixer_w = send(jnp.broadcast_to(slot, (16,) + slot.shape), PLANE).reshape(width, -1)
    w_in = mixer_w[:, : 3 * ch]
    w_out = spread(mixer_w[:, 512:])
    mark_rows = row_back(jnp.eye(8, 128, dtype=BF), mixer_w[:, 384:512])
    gain_one, gain_two = mark_rows[0], mark_rows[1]
    taps = row(mark_rows.astype(BF), order)[2:5]
    taps = lax.dynamic_slice_in_dim(taps, member * ch, ch, axis=1)

    inv_one = lax.rsqrt(jnp.mean(x * x, axis=-1, keepdims=True) + EPS)
    scaled = x * inv_one
    high = lax.reduce_precision(scaled, 8, 7)
    high, low = high.astype(BF), (scaled - high).astype(BF)
    both = box_rows(jnp.concatenate([high, low, cot.astype(BF)], axis=1))
    scaled_all = both[:, :width].astype(F32) + both[:, width : 2 * width].astype(F32)
    cot_all = both[:, 2 * width :]
    n1 = (scaled_all * gain_one).astype(BF)
    mixed = row(n1, w_in)
    gate_b, gate_c, values = mixed[:, :ch], mixed[:, ch : 2 * ch], mixed[:, 2 * ch :]
    gated = gate_b * values

    place = jnp.arange(8)
    its_z = place % 4
    its_core = jnp.where(place < 4, core, 1 - core)
    its_seq, its_turn = its_z % 2, its_z // 2 * 2 + its_core
    same = its_seq[:, None] == its_seq[None, :]
    before = (same & (its_turn[:, None] == its_turn[None, :] + 1)).astype(F32)
    behind = (same & (its_turn[:, None] + 1 == its_turn[None, :])).astype(F32)
    seqs = jnp.arange(2)
    first = ((seqs[:, None] == its_seq[None, :]) & (its_turn[None, :] == 0)).astype(F32)
    last = ((seqs[:, None] == its_seq[None, :]) & (its_turn[None, :] == 3)).astype(F32)

    def pick(table, value):
        return jnp.sum(table[:, :, None, None] * value[None], axis=1)

    def blocks(value):
        return value.reshape(8, rows, -1)

    def halves(product, left, right):
        cut = 4 * rows
        give = product(left[cut:], right, BF)
        return product(left[:cut], right), give

    def flat(value):
        return value.reshape(8 * rows, -1)

    line = [(i, i + 1) for i in range(15)]
    gated_b = blocks(gated)
    ends = gated_b[:, rows - 2 :]
    carried = lax.ppermute(pick(last, ends), PLANE, line)
    heads = pick(before, ends) + pick(first.T, carried)
    late2 = flat(jnp.concatenate([heads, gated_b[:, : rows - 2]], axis=1))
    late1 = flat(jnp.concatenate([heads[:, 1:], gated_b[:, : rows - 1]], axis=1))
    conv = taps[0] * late2 + taps[1] * late1 + taps[2] * gated
    mixer = (gate_c * conv).astype(BF)
    hidden = x + mine(*halves(row, mixer, w_out))
    inv_two = lax.rsqrt(jnp.mean(hidden * hidden, axis=-1, keepdims=True) + EPS)
    n2 = everyone((hidden * inv_two * gain_two).astype(BF))
    w_gu = ffn_w[:, :1280]
    down_most = ffn_w[:, 1280:1792].reshape(16, 2, 32, 512).transpose(0, 2, 1, 3)
    w_down = jnp.concatenate(
        [down_most.reshape(512, width), spread(ffn_w[:, 1792:])], axis=0
    )
    gu = row(n2, w_gu)
    gate_pre, up_pre = gu[:, :640], gu[:, 640:]
    sigma = jax.nn.sigmoid(gate_pre)
    act = (gate_pre * sigma * up_pre).astype(BF)

    grad_act = row_back(cot_all, w_down)
    grad_up_pre = (grad_act * gate_pre * sigma).astype(BF)
    grad_gate_pre = (grad_act * up_pre * sigma * (1.0 + gate_pre * (1.0 - sigma))).astype(BF)
    grad_gu_pre = jnp.concatenate([grad_gate_pre, grad_up_pre], axis=1)
    gn2_part = row_back(grad_gu_pre, w_gu)
    gn2 = mine(gn2_part[: 4 * rows], gn2_part[4 * rows :])
    down_terms = col_sum(act, cot_all)
    down_most = down_terms[:512].reshape(16, 32, 2, 512).transpose(0, 2, 1, 3)
    ffn_sums = jnp.concatenate(
        [col_sum(n2, grad_gu_pre), down_most.reshape(width, 512), stacked(down_terms[512:])],
        axis=1,
    )
    ffn_sums_y = lax.psum_scatter(ffn_sums, "y", scatter_dimension=0, tiled=True)
    ffn_sums = lax.psum_scatter(ffn_sums_y, "x", scatter_dimension=0, tiled=True)
    gain_two_term = jnp.sum(gn2 * hidden * inv_two, axis=0)
    weighted = gn2 * gain_two
    grad_hidden = (
        cot
        + inv_two * weighted
        - hidden * inv_two**3 * jnp.mean(hidden * weighted, axis=-1, keepdims=True)
    )
    hb = everyone(grad_hidden.astype(BF))
    grad_mixer = row_back(hb, w_out)
    grad_c = grad_mixer * conv
    grad_conv = grad_mixer * gate_c
    taps_term = jnp.stack(
        [
            jnp.sum(late2 * grad_conv, axis=0),
            jnp.sum(late1 * grad_conv, axis=0),
            jnp.sum(gated * grad_conv, axis=0),
        ],
        axis=0,
    )
    gc = blocks(grad_conv)
    starts = gc[:, :2]
    from_next = lax.ppermute(pick(first, starts), PLANE, [(b, a) for a, b in line])
    tails = pick(behind, starts) + pick(last.T, from_next)
    lead1 = flat(jnp.concatenate([gc[:, 1:], tails[:, :1]], axis=1))
    lead2 = flat(jnp.concatenate([gc[:, 2:], tails], axis=1))
    grad_gated = taps[2] * grad_conv + taps[1] * lead1 + taps[0] * lead2
    grad_mixed = jnp.concatenate(
        [grad_gated * values, grad_c, grad_gated * gate_b], axis=1
    ).astype(BF)
    keep, give = halves(row_back, grad_mixed, w_in)
    gain_one_term = jnp.sum(keep * scaled_all[: 4 * rows], axis=0)
    gain_one_term += jnp.sum(give.astype(F32) * scaled_all[4 * rows :], axis=0)
    taps_all = jnp.where(jnp.arange(width) // ch == member, jnp.tile(taps_term, (1, 8)), 0.0)
    taps_all = row_back(taps_all.astype(BF), order)
    mark_terms = jnp.concatenate([gain_one_term[None], gain_two_term[None], taps_all], axis=0)
    mark_terms = jnp.pad(mark_terms, ((0, 3), (0, 0))).T
    mark_terms = jnp.pad(mark_terms, ((0, 0), (0, 120))).astype(BF)
    in_terms = col_sum(n1, grad_mixed)
    mixer_terms = jnp.concatenate(
        [in_terms, mark_terms, stacked(col_sum(mixer, hb))], axis=1
    )
    parts = send(mixer_terms.reshape(16, 64, -1), PLANE)
    mixer_sums = jnp.sum(parts.astype(F32), axis=0)
    ffn = after(row(act, w_down), hb)
    late = ffn[: 4 * rows], ffn[4 * rows :].astype(BF)
    gn1, ffn = mine_both((keep, after(give, in_terms)), late, ffn_sums_y)
    weighted = gn1 * gain_one
    input_grad = (
        grad_hidden
        + inv_one * weighted
        - x * inv_one**3 * jnp.mean(x * weighted, axis=-1, keepdims=True)
    )
    result = hidden + ffn

    cols = jnp.concatenate([mixer_sums[:, :512].astype(BF), ffn_sums[:, :1280]], axis=1)
    cols = send(cols.reshape(8, shard, -1), BOX)
    in_cols = cols[:, :, : 3 * ch].reshape(8, shard, 3, ch).transpose(1, 2, 0, 3)
    grad_in = row_back(in_cols.reshape(3 * shard, width), order).reshape(shard, 3 * width)
    mark_sums = jnp.sum(cols[:, :, 384:392].astype(F32), axis=0)
    gu_cols = cols[:, :, 512:].reshape(8, shard, 2, 640)
    most = gu_cols[..., :512].reshape(8, shard, 2, 4, 128).transpose(2, 1, 3, 0, 4)
    rest = gu_cols[..., 512:].reshape(8, shard, 2, 4, 32).transpose(2, 1, 3, 0, 4)
    gu_cols = jnp.concatenate(
        [most.reshape(8 * shard, 1024), rest.reshape(8 * shard, 256)], axis=1
    )
    grad_gate, grad_up = row_back(gu_cols, units).reshape(2, shard, 4608)
    down_most = ffn_sums[:, 1280:1792]
    grad_down = jnp.concatenate(
        [
            jnp.concatenate([down_most[:32], down_most[32:]], axis=1),
            spread(ffn_sums[:, 1792:])[:4],
        ],
        axis=0,
    ).astype(F32)
    shape_rows = block_input.shape
    return (
        result.reshape(shape_rows),
        input_grad.reshape(shape_rows),
        mark_sums[:, 0],
        grad_in,
        mark_sums[:, 2:5],
        spread(mixer_sums[:, 512:]),
        mark_sums[:, 1],
        grad_gate,
        grad_up,
        grad_down,
    )


def solution(mesh):
    torus = Mesh(mesh.devices.reshape(DIMS), AXES)
    line = P("zl", ("y", "x", "zh", "core"), None)
    flat, table = P(AXES), P(AXES, None)
    return jax.shard_map(
        on_device,
        mesh=torus,
        in_specs=(line, flat, table, table, table, flat, table, table, table, line),
        out_specs=(line, line, flat, table, table, table, flat, table, table, table),
        check_vma=False,
    )
```
